512 devices in a mesh: row: 32 (over y, x, core), col: 16 (over z).
Axes of the slice: x: 4, y: 4, z: 16, core: 2. Of those that a mesh axis runs over, the one named last changes fastest.
Arguments:
- matrix: bfloat16 [16384, 16, 2, 512], P('row', 'col'), as said below
- inverses: float32 [2, 512, 512], replicated, as said below
Outputs:
- factored: bfloat16 [16384, 16, 2, 512], P('row', 'col')
Inputs may be any that keep to these rules, and one draw needn't show every extreme that they name: Entries off the diagonal of the whole matrix lie within [-6, 6]; its diagonal entries lie between 3.2 * sqrt(512) and 5 * sqrt(512). Each inverses[s] has diagonal entries between 0.7 and 1.3 times 1 / (4 sqrt(512)) and off-diagonal entries at most 0.4 / 2048 in magnitude.
All inputs are finite; a program needn't handle non-finite values.
Results may differ from the reference program's by a relative error of at most 0.0035.
Values may be sent and summed in bfloat16 or wider, within the bound.
No kernel may reach another device: no remote copies, remote signals or barrier semaphores. Data moves between devices by JAX's collectives and lax.ppermute only.
A program may use at most 64 MiB of HBM per device.

```python
import math
import jax
import jax.numpy as jnp
from jax import lax

NB = 512
STEPS = 2
M = 16384
CB = 2
N_COL = 16


def draw_matrix(key, part):
    key = jax.random.fold_in(key, 11)
    key_body, key_diag = jax.random.split(key)
    shape = (M, N_COL, CB, NB)
    values = jax.random.truncated_normal(key_body, -6.0, 6.0, shape, jnp.float32)
    diag_vals = jax.random.uniform(key_diag, (M, 1, 1, 1), jnp.float32, 0.8, 1.25)
    row_ids = jnp.arange(M, dtype=jnp.int32)[:, None, None, None]
    col_ids = (jnp.arange(CB, dtype=jnp.int32)[None, None, :, None] * N_COL + jnp.arange(N_COL, dtype=jnp.int32)[None, :, None, None]) * NB + jnp.arange(NB, dtype=jnp.int32)[None, None, None, :]
    scaled = diag_vals * (4.0 * math.sqrt(NB))
    return jnp.where(row_ids == col_ids, scaled, values).astype(jnp.bfloat16)


def draw_inverses(key, part):
    key = jax.random.fold_in(key, 23)
    key_gain, key_rest = jax.random.split(key)
    base = 1.0 / (4.0 * math.sqrt(NB))
    gains = jax.random.uniform(key_gain, (STEPS, NB, 1), jnp.float32, 0.7, 1.3)
    spread = jax.random.truncated_normal(key_rest, -4.0, 4.0, (STEPS, NB, NB), jnp.float32)
    rows_idx = jnp.arange(NB, dtype=jnp.int32)[None, :, None]
    cols_idx = jnp.arange(NB, dtype=jnp.int32)[None, None, :]
    others = spread * (0.1 * base / math.sqrt(NB))
    return jnp.where(rows_idx == cols_idx, gains * base, others).astype(jnp.float32)


def setup_inputs(seed: int = 0) -> dict:
    keys = jax.random.split(jax.random.key(seed), 3)
    return {
        "matrix": draw_matrix(jax.random.fold_in(keys[2], 71), 0),
        "inverses": draw_inverses(jax.random.fold_in(keys[2], 71), 0),
    }


def reference(matrix, inverses):
    order = matrix.shape[0]
    working = jnp.transpose(matrix.astype(jnp.float32), (0, 2, 1, 3)).reshape(order, order)
    identity = jnp.eye(NB, dtype=jnp.float32)
    for step_index in range(STEPS):
        low_edge = step_index * NB
        high_edge = (step_index + 1) * NB
        upper = working[low_edge:high_edge, :].astype(jnp.bfloat16)
        diagonal = upper[:, low_edge:high_edge].astype(jnp.float32)
        approx = inverses[step_index]
        product = jnp.dot(diagonal, approx, precision=lax.Precision.HIGHEST)
        inverse = jnp.dot(approx, 2.0 * identity - product, precision=lax.Precision.HIGHEST).astype(jnp.bfloat16)
        lower = jnp.dot(working[high_edge:, low_edge:high_edge], inverse.astype(jnp.float32), precision=lax.Precision.HIGHEST).astype(jnp.bfloat16)
        trailing = working[high_edge:, high_edge:] - jnp.dot(lower, upper[:, high_edge:], preferred_element_type=jnp.float32)
        working = working.at[high_edge:, high_edge:].set(trailing)
        working = working.at[high_edge:, low_edge:high_edge].set(lower.astype(jnp.float32))
    result = working.astype(jnp.bfloat16).reshape(order, CB, N_COL, NB)
    return jnp.transpose(result, (0, 2, 1, 3))
```

```python
import jax
import jax.numpy as jnp
from jax import lax
from jax.sharding import PartitionSpec as P

highest = lax.Precision.HIGHEST


def refined_inverse(diagonal, approx):
    identity = jnp.eye(diagonal.shape[0], dtype=jnp.float32)
    product = jnp.dot(diagonal.astype(jnp.float32), approx, precision=highest)
    return jnp.dot(approx, 2.0 * identity - product, precision=highest).astype(jnp.bfloat16)


def minus_product(base, left, right):
    return base.astype(jnp.float32) - jnp.dot(left, right, preferred_element_type=jnp.float32)


def panel_tree(panel, cols):
    held = panel
    col = lax.axis_index("col")
    reach = cols // 2
    while reach >= 2:
        step = 2 * reach
        pairs = [(s, (s - reach) % cols) for s in range(0, cols, step)]
        pairs += [(s + 1, (s + 1 + reach) % cols) for s in range(0, cols, step)]
        got = lax.ppermute(held, "col", pairs)
        holds = ((col - col % 2) % step) == 0
        held = jnp.where(holds, held, got)
        reach //= 2
    pairs = [(s, (s - 1) % cols) if s % 2 == 0 else (s, (s + 1) % cols) for s in range(cols)]
    other = lax.ppermute(held, "col", pairs)
    even = col % 2 == 0
    return jnp.where(even, held, other), jnp.where(even, other, held)


def spread_diagonal(piece, cols):
    col = lax.axis_index("col")
    quarter = cols // 4
    got = [
        lax.ppermute(piece, "col", [(0, quarter * k), (1, quarter * k + 1)]) for k in range(1, 4)
    ]
    held = jnp.where(col < 2, piece, got[0] + got[1] + got[2])
    groups = range(0, cols, 4)
    swap = lax.ppermute(held, "col", [p for g in groups for p in ((g, g + 1), (g + 1, g))])
    near = lax.ppermute(held, "col", [p for g in groups for p in ((g, g + 2), (g + 1, g + 3))])
    far = lax.ppermute(held, "col", [p for g in groups for p in ((g, g + 3), (g + 1, g + 2))])
    place = col % 4
    first = jnp.where(place == 0, held, jnp.where(place == 1, swap, jnp.where(place == 2, near, far)))
    second = jnp.where(place == 0, swap, jnp.where(place == 1, held, jnp.where(place == 2, far, near)))
    return jnp.stack([first, second])


def local(matrix, inverses):
    rows, cols = lax.axis_size("row"), lax.axis_size("col")
    row, col = lax.axis_index("row"), lax.axis_index("col")
    size = matrix.shape[0]
    chips = rows // 2
    part = size // chips
    same_core = [[2 * chip + core for chip in range(chips)] for core in range(2)]
    swap_core = [(r, r ^ 1) for r in range(rows)]
    core = row % 2

    with jax.named_scope("panels"):
        panel0, panel1 = panel_tree(matrix[:, 0, 0, :], cols)

    with jax.named_scope("scatter_rows"):
        dealt = lax.all_to_all(
            matrix, "row", 0, 0, tiled=True, axis_index_groups=same_core
        )[:part, 0]
    with jax.named_scope("gather_rows"):
        upper = lax.all_gather(dealt.reshape(part, -1), "row", axis=0, tiled=False)
        upper = upper.reshape(chips, 2, part, -1)
        upper0 = upper[:, 0].reshape(size, -1)
        raw1 = upper[:, 1].reshape(size, -1)
    with jax.named_scope("diagonal"):
        pieces = spread_diagonal(dealt[:, 0, :], cols)
        copies = jnp.broadcast_to(pieces[None], (chips,) + pieces.shape)
        mine = lax.all_to_all(copies, "row", 0, 0, tiled=True, axis_index_groups=same_core)
        other = lax.ppermute(mine, "row", swap_core)
        top = jnp.where(core == 0, mine, other)
        low = jnp.where(core == 0, other, mine)
        d00, d01 = (top[:, k].reshape(size, size) for k in range(2))
        d10, d11 = (low[:, k].reshape(size, size) for k in range(2))
    with jax.named_scope("inverses"):
        inverse0 = refined_inverse(d00, inverses[0])
        lower10 = jnp.dot(d10, inverse0, preferred_element_type=jnp.float32).astype(jnp.bfloat16)
        upper11 = minus_product(d11, lower10, d01).astype(jnp.bfloat16)
        inverse1 = refined_inverse(upper11, inverses[1])
    with jax.named_scope("update"):
        upper1 = minus_product(raw1, lower10, upper0).astype(jnp.bfloat16)
        lower0 = jnp.dot(panel0, inverse0, preferred_element_type=jnp.float32).astype(jnp.bfloat16)
        lower1 = jnp.dot(
            minus_product(panel1, lower0, d01), inverse1.astype(jnp.float32), precision=highest
        ).astype(jnp.bfloat16)
        zero = jnp.zeros_like(lower0)
        used0 = jnp.where(row > 0, lower0, zero)
        used1 = jnp.where(row > 1, lower1, zero)
        fresh = minus_product(matrix.reshape(size, -1), used0, upper0)
        fresh = fresh - jnp.dot(used1, upper1, preferred_element_type=jnp.float32)
        fresh = fresh.astype(jnp.bfloat16).reshape(size, 2, size)
        head = fresh[:, 0]
        head = jnp.where((col == 0) & (row > 0), lower0, head)
        head = jnp.where((col == 1) & (row > 1), lower1, head)
        return jnp.stack([head, fresh[:, 1]], axis=1)[:, None]


def solution(mesh):
    return jax.shard_map(
        local,
        mesh=mesh,
        in_specs=(P("row", "col", None, None), P()),
        out_specs=P("row", "col", None, None),
        check_vma=False,
    )
```

```python
import jax
import jax.numpy as jnp
from jax import lax
from jax.sharding import PartitionSpec as P

highest = lax.Precision.HIGHEST


def refined_inverse(diagonal, approx):
    identity = jnp.eye(diagonal.shape[0], dtype=jnp.float32)
    product = jnp.dot(diagonal.astype(jnp.float32), approx, precision=highest)
    return jnp.dot(approx, 2.0 * identity - product, precision=highest).astype(jnp.bfloat16)


def minus_product(base, left, right):
    return base.astype(jnp.float32) - jnp.dot(left, right, preferred_element_type=jnp.float32)


def panel_step(held, reach, cols):
    col = lax.axis_index("col")
    step = 2 * reach
    pairs = [(s, (s - reach) % cols) for s in range(0, cols, step)]
    pairs += [(s + 1, (s + 1 + reach) % cols) for s in range(0, cols, step)]
    got = lax.ppermute(held, "col", pairs)
    return jnp.where((col - col % 2) % step == 0, held, got)


def panel_pair(held, cols):
    even = lax.axis_index("col") % 2 == 0
    pairs = [(s, (s - 1) % cols) if s % 2 == 0 else (s, (s + 1) % cols) for s in range(cols)]
    other = lax.ppermute(held, "col", pairs)
    return jnp.where(even, held, other), jnp.where(even, other, held)


def spread_diagonal(piece, cols):
    col = lax.axis_index("col")
    quarter = cols // 4
    got = [
        lax.ppermute(piece, "col", [(0, quarter * k), (1, quarter * k + 1)]) for k in range(1, 4)
    ]
    held = jnp.where(col < 2, piece, got[0] + got[1] + got[2])
    groups = range(0, cols, 4)
    swap = lax.ppermute(held, "col", [p for g in groups for p in ((g, g + 1), (g + 1, g))])
    near = lax.ppermute(held, "col", [p for g in groups for p in ((g, g + 2), (g + 1, g + 3))])
    far = lax.ppermute(held, "col", [p for g in groups for p in ((g, g + 3), (g + 1, g + 2))])
    place = col % 4
    first = jnp.where(place == 0, held, jnp.where(place == 1, swap, jnp.where(place == 2, near, far)))
    second = jnp.where(place == 0, swap, jnp.where(place == 1, held, jnp.where(place == 2, far, near)))
    return jnp.stack([first, second])


def local(matrix, inverses):
    rows, cols = lax.axis_size("row"), lax.axis_size("col")
    row, col = lax.axis_index("row"), lax.axis_index("col")
    size = matrix.shape[0]
    chips = rows // 2
    part = size // chips
    same_core = [[2 * chip + core for chip in range(chips)] for core in range(2)]
    swap_core = [(r, r ^ 1) for r in range(rows)]
    core = row % 2

    def gather_part(piece):
        copies = jnp.broadcast_to(piece[None], (chips,) + piece.shape)
        return lax.all_to_all(copies, "row", 0, 0, tiled=True, axis_index_groups=same_core)

    with jax.named_scope("panels"):
        held = panel_step(matrix[:, 0, 0, :], 8, cols)
    with jax.named_scope("scatter_rows"):
        dealt = lax.all_to_all(
            matrix, "row", 0, 0, tiled=True, axis_index_groups=same_core
        )[:part, 0]
    dealt, held = lax.optimization_barrier((dealt, held))
    with jax.named_scope("panels"):
        held = panel_step(held, 4, cols)
    with jax.named_scope("diagonal"):
        pieces = spread_diagonal(dealt[:, 0, :], cols)
        pieces, held = lax.optimization_barrier((pieces, held))
    with jax.named_scope("panels"):
        held = panel_step(held, 2, cols)
    with jax.named_scope("diagonal"):
        mine = gather_part(pieces)
        mine, held = lax.optimization_barrier((mine, held))
    with jax.named_scope("panels"):
        panel0, panel1 = panel_pair(held, cols)
    with jax.named_scope("diagonal"):
        other = lax.ppermute(mine, "row", swap_core)
        top = jnp.where(core == 0, mine, other)
        low = jnp.where(core == 0, other, mine)
        d00, d01 = (top[:, k].reshape(size, size) for k in range(2))
        d10, d11 = (low[:, k].reshape(size, size) for k in range(2))
    with jax.named_scope("gather_rows"):
        own_rows = gather_part(dealt.reshape(part, -1)).reshape(size, -1)
        own_rows, panel0, panel1 = lax.optimization_barrier((own_rows, panel0, panel1))
        other_rows = lax.ppermute(own_rows, "row", swap_core)
        upper0 = jnp.where(core == 0, own_rows, other_rows)
        raw1 = jnp.where(core == 0, other_rows, own_rows)
    with jax.named_scope("inverses"):
        inverse0 = refined_inverse(d00, inverses[0])
        lower10 = jnp.dot(d10, inverse0, preferred_element_type=jnp.float32).astype(jnp.bfloat16)
        upper11 = minus_product(d11, lower10, d01).astype(jnp.bfloat16)
        inverse1 = refined_inverse(upper11, inverses[1])
    with jax.named_scope("update"):
        upper1 = minus_product(raw1, lower10, upper0).astype(jnp.bfloat16)
        lower0 = jnp.dot(panel0, inverse0, preferred_element_type=jnp.float32).astype(jnp.bfloat16)
        lower1 = jnp.dot(
            minus_product(panel1, lower0, d01), inverse1.astype(jnp.float32), precision=highest
        ).astype(jnp.bfloat16)
        zero = jnp.zeros_like(lower0)
        used0 = jnp.where(row > 0, lower0, zero)
        used1 = jnp.where(row > 1, lower1, zero)
        fresh = minus_product(matrix.reshape(size, -1), used0, upper0)
        fresh = fresh - jnp.dot(used1, upper1, preferred_element_type=jnp.float32)
        fresh = fresh.astype(jnp.bfloat16).reshape(size, 2, size)
        head = fresh[:, 0]
        head = jnp.where((col == 0) & (row > 0), lower0, head)
        head = jnp.where((col == 1) & (row > 1), lower1, head)
        return jnp.stack([head, fresh[:, 1]], axis=1)[:, None]


def solution(mesh):
    return jax.shard_map(
        local,
        mesh=mesh,
        in_specs=(P("row", "col", None, None), P()),
        out_specs=P("row", "col", None, None),
        check_vma=False,
    )
```

```python
import jax
import jax.numpy as jnp
from jax import lax
from jax.sharding import PartitionSpec as P

highest = lax.Precision.HIGHEST


def refined_inverse(diagonal, approx):
    identity = jnp.eye(diagonal.shape[0], dtype=jnp.float32)
    product = jnp.dot(diagonal.astype(jnp.float32), approx, precision=highest)
    return jnp.dot(approx, 2.0 * identity - product, precision=highest).astype(jnp.bfloat16)


def minus_product(base, left, right):
    return base.astype(jnp.float32) - jnp.dot(left, right, preferred_element_type=jnp.float32)


def panel_step(held, level, cols):
    tree = [[(0, 10)], [(0, 4), (10, 6)], [(0, 14), (4, 2), (6, 8), (10, 12)]][level]
    pairs = tree + [((1 - s) % cols, (1 - t) % cols) for s, t in tree]
    got = lax.ppermute(held, "col", pairs)
    col = lax.axis_index("col")
    arrives = jnp.any(jnp.stack([col == t for _, t in pairs]))
    return jnp.where(arrives, got, held)


def panel_pair(held, cols):
    even = lax.axis_index("col") % 2 == 0
    pairs = [(s, (s - 1) % cols) if s % 2 == 0 else (s, (s + 1) % cols) for s in range(cols)]
    other = lax.ppermute(held, "col", pairs)
    return jnp.where(even, held, other), jnp.where(even, other, held)


def spread_diagonal(piece, cols):
    col = lax.axis_index("col")
    quarter = cols // 4
    got = [
        lax.ppermute(piece, "col", [(0, quarter * k), (1, quarter * k + 1)]) for k in range(1, 4)
    ]
    held = jnp.where(col < 2, piece, got[0] + got[1] + got[2])
    groups = range(0, cols, 4)
    swap = lax.ppermute(held, "col", [p for g in groups for p in ((g, g + 1), (g + 1, g))])
    near = lax.ppermute(held, "col", [p for g in groups for p in ((g, g + 2), (g + 1, g + 3))])
    far = lax.ppermute(held, "col", [p for g in groups for p in ((g, g + 3), (g + 1, g + 2))])
    place = col % 4
    first = jnp.where(place == 0, held, jnp.where(place == 1, swap, jnp.where(place == 2, near, far)))
    second = jnp.where(place == 0, swap, jnp.where(place == 1, held, jnp.where(place == 2, far, near)))
    return jnp.stack([first, second])


def local(matrix, inverses):
    rows, cols = lax.axis_size("row"), lax.axis_size("col")
    row, col = lax.axis_index("row"), lax.axis_index("col")
    size = matrix.shape[0]
    chips = rows // 2
    part = size // chips
    same_core = [[2 * chip + core for chip in range(chips)] for core in range(2)]
    swap_core = [(r, r ^ 1) for r in range(rows)]
    core = row % 2

    def gather_part(piece):
        copies = jnp.broadcast_to(piece[None], (chips,) + piece.shape)
        return lax.all_to_all(copies, "row", 0, 0, tiled=True, axis_index_groups=same_core)

    with jax.named_scope("panels"):
        held = panel_step(matrix[:, 0, 0, :], 0, cols)
    with jax.named_scope("scatter_rows"):
        dealt = lax.all_to_all(
            matrix, "row", 0, 0, tiled=True, axis_index_groups=same_core
        )[:part, 0]
    dealt, held = lax.optimization_barrier((dealt, held))
    with jax.named_scope("panels"):
        held = panel_step(held, 1, cols)
    with jax.named_scope("gather_rows"):
        own_rows = gather_part(dealt.reshape(part, -1)).reshape(size, -1)
    with jax.named_scope("diagonal"):
        pieces = spread_diagonal(dealt[:, 0, :], cols)
        pieces, held, own_rows = lax.optimization_barrier((pieces, held, own_rows))
    with jax.named_scope("gather_rows"):
        other_rows = lax.ppermute(own_rows, "row", swap_core)
        upper0 = jnp.where(core == 0, own_rows, other_rows)
        raw1 = jnp.where(core == 0, other_rows, own_rows)
    with jax.named_scope("panels"):
        held = panel_step(held, 2, cols)
    with jax.named_scope("diagonal"):
        mine = gather_part(pieces)
        mine, held = lax.optimization_barrier((mine, held))
    with jax.named_scope("panels"):
        panel0, panel1 = panel_pair(held, cols)
    with jax.named_scope("diagonal"):
        other = lax.ppermute(mine, "row", swap_core)
        top = jnp.where(core == 0, mine, other)
        low = jnp.where(core == 0, other, mine)
        d00, d01 = (top[:, k].reshape(size, size) for k in range(2))
        d10, d11 = (low[:, k].reshape(size, size) for k in range(2))
    with jax.named_scope("inverses"):
        inverse0 = refined_inverse(d00, inverses[0])
        lower10 = jnp.dot(d10, inverse0, preferred_element_type=jnp.float32).astype(jnp.bfloat16)
        upper11 = minus_product(d11, lower10, d01).astype(jnp.bfloat16)
        inverse1 = refined_inverse(upper11, inverses[1])
    with jax.named_scope("update"):
        upper1 = minus_product(raw1, lower10, upper0).astype(jnp.bfloat16)
        lower0 = jnp.dot(panel0, inverse0, preferred_element_type=jnp.float32).astype(jnp.bfloat16)
        lower1 = jnp.dot(
            minus_product(panel1, lower0, d01), inverse1.astype(jnp.float32), precision=highest
        ).astype(jnp.bfloat16)
        zero = jnp.zeros_like(lower0)
        used0 = jnp.where(row > 0, lower0, zero)
        used1 = jnp.where(row > 1, lower1, zero)
        fresh = minus_product(matrix.reshape(size, -1), used0, upper0)
        fresh = fresh - jnp.dot(used1, upper1, preferred_element_type=jnp.float32)
        fresh = fresh.astype(jnp.bfloat16).reshape(size, 2, size)
        head = fresh[:, 0]
        head = jnp.where((col == 0) & (row > 0), lower0, head)
        head = jnp.where((col == 1) & (row > 1), lower1, head)
        return jnp.stack([head, fresh[:, 1]], axis=1)[:, None]


def solution(mesh):
    return jax.shard_map(
        local,
        mesh=mesh,
        in_specs=(P("row", "col", None, None), P()),
        out_specs=P("row", "col", None, None),
        check_vma=False,
    )
```

```python
import jax
import jax.numpy as jnp
from jax import lax
from jax.experimental import pallas as pl
from jax.experimental.pallas import tpu as pltpu
from jax.sharding import PartitionSpec as P

whole = pl.BlockSpec(memory_space=pltpu.VMEM)
params = pltpu.CompilerParams(vmem_limit_bytes=48 * 1024 * 1024)


def product(left, right):
    return jnp.dot(left, right, preferred_element_type=jnp.float32)


def two_parts(value):
    high = value.astype(jnp.bfloat16)
    return high, (value - high.astype(jnp.float32)).astype(jnp.bfloat16)


def refined_inverse(diagonal, approx):
    size = diagonal.shape[0]
    high, low = two_parts(approx)
    row_ids = lax.broadcasted_iota(jnp.int32, (size, size), 0)
    col_ids = lax.broadcasted_iota(jnp.int32, (size, size), 1)
    twice = jnp.where(row_ids == col_ids, 2.0, 0.0)
    rest_high, rest_low = two_parts(twice - (product(diagonal, high) + product(diagonal, low)))
    small = product(high, rest_low) + product(low, rest_high)
    return (product(high, rest_high) + small).astype(jnp.bfloat16)


def upper_kernel(
    own_diag, other_diag, own_rows, other_rows, approx,
    inverse0_ref, inverse1_ref, corner_ref, upper0_ref, upper1_ref,
):
    first = lax.axis_index("row") % 2 == 0
    size = inverse0_ref.shape[0]

    def block(row, col):
        own, other = own_diag[:, col], other_diag[:, col]
        picked = jnp.where(first, own, other) if row == 0 else jnp.where(first, other, own)
        return picked.reshape(size, size)

    inverse0 = refined_inverse(block(0, 0), approx[0])
    inverse0_ref[...] = inverse0
    corner = block(0, 1)
    corner_ref[...] = corner
    lower10 = product(block(1, 0), inverse0).astype(jnp.bfloat16)
    upper11 = (block(1, 1).astype(jnp.float32) - product(lower10, corner)).astype(jnp.bfloat16)
    inverse1_ref[...] = refined_inverse(upper11, approx[1])
    upper0 = jnp.where(first, own_rows[...], other_rows[...])
    upper0_ref[...] = upper0
    raw1 = jnp.where(first, other_rows[...], own_rows[...])
    upper1_ref[...] = (raw1.astype(jnp.float32) - product(lower10, upper0)).astype(jnp.bfloat16)


def update_kernel(
    held, other, block, inverse0, inverse1, corner, upper0, upper1, out,
):
    row, col = lax.axis_index("row"), lax.axis_index("col")
    even = col % 2 == 0
    size = inverse0.shape[0]
    half = size // 2
    for part in range(2):
        rows = pl.ds(part * half, half)
        panel0 = jnp.where(even, held[rows], other[rows])
        panel1 = jnp.where(even, other[rows], held[rows])
        lower0 = product(panel0, inverse0[...]).astype(jnp.bfloat16)
        rest = panel1.astype(jnp.float32) - product(lower0, corner[...])
        rest_high, rest_low = two_parts(rest)
        lower1 = product(rest_high, inverse1[...]) + product(rest_low, inverse1[...])
        lower1 = lower1.astype(jnp.bfloat16)
        used0 = jnp.where(row > 0, lower0, jnp.zeros_like(lower0))
        used1 = jnp.where(row > 1, lower1, jnp.zeros_like(lower1))
        fresh = block[rows].astype(jnp.float32) - product(used0, upper0[...])
        out[rows] = (fresh - product(used1, upper1[...])).astype(jnp.bfloat16)

        @pl.when((col == 0) & (row > 0))
        def _():
            out[rows, pl.ds(0, size)] = lower0

        @pl.when((col == 1) & (row > 1))
        def _():
            out[rows, pl.ds(0, size)] = lower1


def local_call(kernel, count, shapes):
    return pl.pallas_call(
        kernel,
        out_shape=[jax.ShapeDtypeStruct(shape, jnp.bfloat16) for shape in shapes],
        in_specs=[whole] * count,
        out_specs=[whole] * len(shapes),
        compiler_params=params,
    )


def panel_step(held, level, cols):
    tree = [[(0, 10)], [(0, 4), (10, 6)], [(0, 14), (4, 2), (6, 8), (10, 12)]][level]
    pairs = tree + [((1 - s) % cols, (1 - t) % cols) for s, t in tree]
    got = lax.ppermute(held, "col", pairs)
    col = lax.axis_index("col")
    arrives = jnp.any(jnp.stack([col == t for _, t in pairs]))
    return jnp.where(arrives, got, held)


def panel_pair(held, cols):
    pairs = [(s, (s - 1) % cols) if s % 2 == 0 else (s, (s + 1) % cols) for s in range(cols)]
    return lax.ppermute(held, "col", pairs)


def spread_diagonal(piece, cols):
    col = lax.axis_index("col")
    quarter = cols // 4
    got = [
        lax.ppermute(piece, "col", [(0, quarter * k), (1, quarter * k + 1)]) for k in range(1, 4)
    ]
    held = jnp.where(col < 2, piece, got[0] + got[1] + got[2])
    groups = range(0, cols, 4)
    swap = lax.ppermute(held, "col", [p for g in groups for p in ((g, g + 1), (g + 1, g))])
    near = lax.ppermute(held, "col", [p for g in groups for p in ((g, g + 2), (g + 1, g + 3))])
    far = lax.ppermute(held, "col", [p for g in groups for p in ((g, g + 3), (g + 1, g + 2))])
    place = col % 4
    first = jnp.where(place == 0, held, jnp.where(place == 1, swap, jnp.where(place == 2, near, far)))
    second = jnp.where(place == 0, swap, jnp.where(place == 1, held, jnp.where(place == 2, far, near)))
    return jnp.stack([first, second])


def local(matrix, inverses):
    rows, cols = lax.axis_size("row"), lax.axis_size("col")
    size = matrix.shape[0]
    chips = rows // 2
    part = size // chips
    same_core = [[2 * chip + core for chip in range(chips)] for core in range(2)]
    swap_core = [(r, r ^ 1) for r in range(rows)]

    def gather_part(piece):
        copies = jnp.broadcast_to(piece[None], (chips,) + piece.shape)
        return lax.all_to_all(copies, "row", 0, 0, tiled=True, axis_index_groups=same_core)

    with jax.named_scope("panels"):
        held = panel_step(matrix[:, 0, 0, :], 0, cols)
    with jax.named_scope("scatter_rows"):
        dealt = lax.all_to_all(
            matrix, "row", 0, 0, tiled=True, axis_index_groups=same_core
        )[:part, 0]
    dealt, held = lax.optimization_barrier((dealt, held))
    with jax.named_scope("panels"):
        held = panel_step(held, 1, cols)
    with jax.named_scope("gather_rows"):
        own_rows = gather_part(dealt.reshape(part, -1)).reshape(size, -1)
    with jax.named_scope("diagonal"):
        pieces = spread_diagonal(dealt[:, 0, :], cols)
        pieces, held, own_rows = lax.optimization_barrier((pieces, held, own_rows))
    with jax.named_scope("gather_rows"):
        other_rows = lax.ppermute(own_rows, "row", swap_core)
    with jax.named_scope("panels"):
        held = panel_step(held, 2, cols)
    with jax.named_scope("diagonal"):
        mine = gather_part(pieces)
        mine, held = lax.optimization_barrier((mine, held))
    with jax.named_scope("panels"):
        panel = panel_pair(held, cols)
    with jax.named_scope("diagonal"):
        other = lax.ppermute(mine, "row", swap_core)
    square, wide = (size, size), (size, 2 * size)
    with jax.named_scope("upper"):
        inverse0, inverse1, corner, upper0, upper1 = local_call(
            upper_kernel, 5, [square, square, square, wide, wide]
        )(mine, other, own_rows, other_rows, inverses)
    with jax.named_scope("update"):
        (fresh,) = local_call(update_kernel, 8, [wide])(
            held, panel, matrix.reshape(wide), inverse0, inverse1, corner, upper0, upper1
        )
    return fresh.reshape(matrix.shape)


def solution(mesh):
    return jax.shard_map(
        local,
        mesh=mesh,
        in_specs=(P("row", "col", None, None), P()),
        out_specs=P("row", "col", None, None),
        check_vma=False,
    )
```

```python
import jax
import jax.numpy as jnp
from jax import lax
from jax.experimental import pallas as pl
from jax.experimental.pallas import tpu as pltpu
from jax.sharding import PartitionSpec as P

whole = pl.BlockSpec(memory_space=pltpu.VMEM)
params = pltpu.CompilerParams(vmem_limit_bytes=32 * 1024 * 1024)


def product(left, right):
    return jnp.dot(left, right, preferred_element_type=jnp.float32)


def two_parts(value):
    high = value.astype(jnp.bfloat16)
    return high, (value - high.astype(jnp.float32)).astype(jnp.bfloat16)


def refined_inverse(diagonal, approx):
    size = diagonal.shape[0]
    high, low = two_parts(approx)
    row_ids = lax.broadcasted_iota(jnp.int32, (size, size), 0)
    col_ids = lax.broadcasted_iota(jnp.int32, (size, size), 1)
    twice = jnp.where(row_ids == col_ids, 2.0, 0.0)
    rest_high, rest_low = two_parts(twice - (product(diagonal, high) + product(diagonal, low)))
    small = product(high, rest_low) + product(low, rest_high)
    return (product(high, rest_high) + small).astype(jnp.bfloat16)


def finish_kernel(
    own_diag, other_diag, approx, own_rows, other_rows, held, other, block, out,
    upper0_ref, raw1_ref, panel0_ref, panel1_ref, block_ref, sems,
):
    row, col = lax.axis_index("row"), lax.axis_index("col")
    first, even = row % 2 == 0, col % 2 == 0
    size = out.shape[0]

    def fetch(source, target, index):
        return pltpu.make_async_copy(source, target, sems.at[index])

    @pl.when(first)
    def _():
        fetch(own_rows, upper0_ref, 0).start()
        fetch(other_rows, raw1_ref, 1).start()

    @pl.when(jnp.logical_not(first))
    def _():
        fetch(other_rows, upper0_ref, 0).start()
        fetch(own_rows, raw1_ref, 1).start()

    @pl.when(even)
    def _():
        fetch(held, panel0_ref, 2).start()
        fetch(other, panel1_ref, 3).start()

    @pl.when(jnp.logical_not(even))
    def _():
        fetch(other, panel0_ref, 2).start()
        fetch(held, panel1_ref, 3).start()

    fetch(block, block_ref, 4).start()

    def corner(top, side):
        own, exchanged = own_diag[:, side], other_diag[:, side]
        picked = jnp.where(first, own, exchanged) if top else jnp.where(first, exchanged, own)
        return picked.reshape(size, size)

    inverse0 = refined_inverse(corner(True, 0), approx[0])
    right = corner(True, 1)
    lower10 = product(corner(False, 0), inverse0).astype(jnp.bfloat16)
    upper11 = corner(False, 1).astype(jnp.float32) - product(lower10, right)
    inverse1 = refined_inverse(upper11.astype(jnp.bfloat16), approx[1])
    fetch(own_rows, upper0_ref, 0).wait()
    fetch(own_rows, raw1_ref, 1).wait()
    upper0 = upper0_ref[...]
    upper1 = raw1_ref[...].astype(jnp.float32) - product(lower10, upper0)
    upper1 = upper1.astype(jnp.bfloat16)
    fetch(held, panel0_ref, 2).wait()
    fetch(held, panel1_ref, 3).wait()
    fetch(block, block_ref, 4).wait()
    half = size // 2
    for part in range(2):
        rows = pl.ds(part * half, half)
        lower0 = product(panel0_ref[rows], inverse0).astype(jnp.bfloat16)
        rest = panel1_ref[rows].astype(jnp.float32) - product(lower0, right)
        rest_high, rest_low = two_parts(rest)
        lower1 = product(rest_high, inverse1) + product(rest_low, inverse1)
        lower1 = lower1.astype(jnp.bfloat16)
        used0 = jnp.where(row > 0, lower0, jnp.zeros_like(lower0))
        used1 = jnp.where(row > 1, lower1, jnp.zeros_like(lower1))
        fresh = block_ref[rows].astype(jnp.float32) - product(used0, upper0)
        out[rows] = (fresh - product(used1, upper1)).astype(jnp.bfloat16)

        @pl.when((col == 0) & (row > 0))
        def _():
            out[rows, pl.ds(0, size)] = lower0

        @pl.when((col == 1) & (row > 1))
        def _():
            out[rows, pl.ds(0, size)] = lower1


def panel_step(held, level, cols):
    tree = [[(0, 10)], [(0, 4), (10, 6)], [(0, 14), (4, 2), (6, 8), (10, 12)]][level]
    pairs = tree + [((1 - s) % cols, (1 - t) % cols) for s, t in tree]
    got = lax.ppermute(held, "col", pairs)
    col = lax.axis_index("col")
    arrives = jnp.any(jnp.stack([col == t for _, t in pairs]))
    return jnp.where(arrives, got, held)


def panel_pair(held, cols):
    pairs = [(s, (s - 1) % cols) if s % 2 == 0 else (s, (s + 1) % cols) for s in range(cols)]
    return lax.ppermute(held, "col", pairs)


def deal_rows(block, chips):
    chip, side = lax.axis_index("row") // 2, 4
    lanes = chips // side
    part = block.shape[0] // lanes
    got = [
        lax.ppermute(
            block[k * part : (k + 1) * part], "row", [(c, 2 * side * k + c) for c in range(2)]
        )
        for k in range(1, lanes)
    ]
    quarter = jnp.where(chip // side == 0, block[:part], sum(got[1:], got[0]))
    small = part // side
    got = [
        lax.ppermute(
            quarter[k * small : (k + 1) * small],
            "row",
            [(2 * side * y + c, 2 * (side * y + k) + c) for y in range(lanes) for c in range(2)],
        )
        for k in range(1, side)
    ]
    return jnp.where(chip % side == 0, quarter[:small], sum(got[1:], got[0]))


def spread_far(piece, cols):
    quarter = cols // 4
    got = [
        lax.ppermute(piece, "col", [(0, quarter * k), (1, quarter * k + 1)]) for k in range(1, 4)
    ]
    return jnp.where(lax.axis_index("col") < 2, piece, got[0] + got[1] + got[2])


def spread_near(held, cols):
    groups = range(0, cols, 4)
    swap = lax.ppermute(held, "col", [p for g in groups for p in ((g, g + 1), (g + 1, g))])
    near = lax.ppermute(held, "col", [p for g in groups for p in ((g, g + 2), (g + 1, g + 3))])
    far = lax.ppermute(held, "col", [p for g in groups for p in ((g, g + 3), (g + 1, g + 2))])
    place = lax.axis_index("col") % 4
    first = jnp.where(place == 0, held, jnp.where(place == 1, swap, jnp.where(place == 2, near, far)))
    second = jnp.where(place == 0, swap, jnp.where(place == 1, held, jnp.where(place == 2, far, near)))
    return jnp.stack([first, second])


def local(matrix, inverses):
    rows, cols = lax.axis_size("row"), lax.axis_size("col")
    size = matrix.shape[0]
    chips = rows // 2
    part = size // chips
    same_core = [[2 * chip + core for chip in range(chips)] for core in range(2)]
    swap_core = [(r, r ^ 1) for r in range(rows)]

    def gather_part(piece):
        copies = jnp.broadcast_to(piece[None], (chips,) + piece.shape)
        return lax.all_to_all(copies, "row", 0, 0, tiled=True, axis_index_groups=same_core)

    with jax.named_scope("panels"):
        held = panel_step(matrix[:, 0, 0, :], 0, cols)
    with jax.named_scope("scatter_rows"):
        dealt = lax.all_to_all(
            matrix, "row", 0, 0, tiled=True, axis_index_groups=same_core
        )[:part, 0]
    first_dealt = dealt
    with jax.named_scope("panels"):
        held = panel_step(held, 1, cols)
    dealt, held = lax.optimization_barrier((dealt, held))
    with jax.named_scope("gather_rows"):
        own_rows = gather_part(first_dealt.reshape(part, -1)).reshape(size, -1)
    with jax.named_scope("diagonal"):
        piece = spread_far(dealt[:, 0, :], cols)
    piece, own_rows, held = lax.optimization_barrier((piece, own_rows, held))
    with jax.named_scope("panels"):
        held = panel_step(held, 2, cols)
    with jax.named_scope("diagonal"):
        pieces = spread_near(piece, cols)
    pieces, held = lax.optimization_barrier((pieces, held))
    with jax.named_scope("gather_rows"):
        other_rows = lax.ppermute(own_rows, "row", swap_core)
    with jax.named_scope("diagonal"):
        mine = gather_part(pieces)
    with jax.named_scope("panels"):
        panel = panel_pair(held, cols)
    mine, panel = lax.optimization_barrier((mine, panel))
    late, mine = lax.optimization_barrier((matrix, mine))
    with jax.named_scope("diagonal"):
        other = lax.ppermute(mine, "row", swap_core)
    wide = (size, 2 * size)
    with jax.named_scope("finish"):
        fresh = pl.pallas_call(
            finish_kernel,
            out_shape=jax.ShapeDtypeStruct(wide, jnp.bfloat16),
            in_specs=[whole] * 3 + [pl.BlockSpec(memory_space=pl.ANY)] * 5,
            out_specs=whole,
            scratch_shapes=[pltpu.VMEM(wide, jnp.bfloat16)] * 2
            + [pltpu.VMEM((size, size), jnp.bfloat16)] * 2
            + [pltpu.VMEM(wide, jnp.bfloat16), pltpu.SemaphoreType.DMA((5,))],
            compiler_params=params,
        )(mine, other, inverses, own_rows, other_rows, held, panel, late.reshape(wide))
    return fresh.reshape(matrix.shape)


def solution(mesh):
    return jax.shard_map(
        local,
        mesh=mesh,
        in_specs=(P("row", "col", None, None), P()),
        out_specs=P("row", "col", None, None),
        check_vma=False,
    )
```

```python
import jax
import jax.numpy as jnp
from jax import lax
from jax.experimental import pallas as pl
from jax.experimental.pallas import tpu as pltpu
from jax.sharding import PartitionSpec as P

whole = pl.BlockSpec(memory_space=pltpu.VMEM)
params = pltpu.CompilerParams(vmem_limit_bytes=32 * 1024 * 1024)


def product(left, right):
    return jnp.dot(left, right, preferred_element_type=jnp.float32)


def two_parts(value):
    high = value.astype(jnp.bfloat16)
    return high, (value - high.astype(jnp.float32)).astype(jnp.bfloat16)


def refined_inverse(diagonal, approx):
    size = diagonal.shape[0]
    high, low = two_parts(approx)
    row_ids = lax.broadcasted_iota(jnp.int32, (size, size), 0)
    col_ids = lax.broadcasted_iota(jnp.int32, (size, size), 1)
    twice = jnp.where(row_ids == col_ids, 2.0, 0.0)
    rest_high, rest_low = two_parts(twice - (product(diagonal, high) + product(diagonal, low)))
    small = product(high, rest_low) + product(low, rest_high)
    return (product(high, rest_high) + small).astype(jnp.bfloat16)


def finish_kernel(
    own_diag, other_diag, approx, own_rows, other_rows, held, other, block, out,
    upper0_ref, raw1_ref, panel0_ref, panel1_ref, block_ref, sems,
):
    row, col = lax.axis_index("row"), lax.axis_index("col")
    first, even = row % 2 == 0, col % 2 == 0
    size = out.shape[0]

    def fetch(source, target, index):
        return pltpu.make_async_copy(source, target, sems.at[index])

    @pl.when(first)
    def _():
        fetch(own_rows, upper0_ref, 0).start()
        fetch(other_rows, raw1_ref, 1).start()

    @pl.when(jnp.logical_not(first))
    def _():
        fetch(other_rows, upper0_ref, 0).start()
        fetch(own_rows, raw1_ref, 1).start()

    @pl.when(even)
    def _():
        fetch(held, panel0_ref, 2).start()
        fetch(other, panel1_ref, 3).start()

    @pl.when(jnp.logical_not(even))
    def _():
        fetch(other, panel0_ref, 2).start()
        fetch(held, panel1_ref, 3).start()

    fetch(block, block_ref, 4).start()

    def corner(top, side):
        own, exchanged = own_diag[:, side], other_diag[:, side]
        picked = jnp.where(first, own, exchanged) if top else jnp.where(first, exchanged, own)
        return picked.reshape(size, size)

    inverse0 = refined_inverse(corner(True, 0), approx[0])
    right = corner(True, 1)
    lower10 = product(corner(False, 0), inverse0).astype(jnp.bfloat16)
    upper11 = corner(False, 1).astype(jnp.float32) - product(lower10, right)
    inverse1 = refined_inverse(upper11.astype(jnp.bfloat16), approx[1])
    fetch(own_rows, upper0_ref, 0).wait()
    fetch(own_rows, raw1_ref, 1).wait()
    upper0 = upper0_ref[...]
    upper1 = raw1_ref[...].astype(jnp.float32) - product(lower10, upper0)
    upper1 = upper1.astype(jnp.bfloat16)
    fetch(held, panel0_ref, 2).wait()
    fetch(held, panel1_ref, 3).wait()
    fetch(block, block_ref, 4).wait()
    half = size // 2
    for part in range(2):
        rows = pl.ds(part * half, half)
        lower0 = product(panel0_ref[rows], inverse0).astype(jnp.bfloat16)
        rest = panel1_ref[rows].astype(jnp.float32) - product(lower0, right)
        rest_high, rest_low = two_parts(rest)
        lower1 = product(rest_high, inverse1) + product(rest_low, inverse1)
        lower1 = lower1.astype(jnp.bfloat16)
        used0 = jnp.where(row > 0, lower0, jnp.zeros_like(lower0))
        used1 = jnp.where(row > 1, lower1, jnp.zeros_like(lower1))
        fresh = block_ref[rows].astype(jnp.float32) - product(used0, upper0)
        out[rows] = (fresh - product(used1, upper1)).astype(jnp.bfloat16)

        @pl.when((col == 0) & (row > 0))
        def _():
            out[rows, pl.ds(0, size)] = lower0

        @pl.when((col == 1) & (row > 1))
        def _():
            out[rows, pl.ds(0, size)] = lower1


def panel_step(held, level, cols):
    tree = [[(0, 10)], [(0, 12), (10, 4)], [(0, 2), (4, 6), (10, 8), (12, 14)]][level]
    pairs = tree + [((1 - s) % cols, (1 - t) % cols) for s, t in tree]
    got = lax.ppermute(held, "col", pairs)
    col = lax.axis_index("col")
    arrives = jnp.any(jnp.stack([col == t for _, t in pairs]))
    return jnp.where(arrives, got, held)


def panel_pair(held, cols):
    pairs = [(s, (s - 1) % cols) if s % 2 == 0 else (s, (s + 1) % cols) for s in range(cols)]
    return lax.ppermute(held, "col", pairs)


def deal_rows(block, chips):
    chip, side = lax.axis_index("row") // 2, 4
    lanes = chips // side
    part = block.shape[0] // lanes
    got = [
        lax.ppermute(
            block[k * part : (k + 1) * part], "row", [(c, 2 * side * k + c) for c in range(2)]
        )
        for k in range(1, lanes)
    ]
    quarter = jnp.where(chip // side == 0, block[:part], sum(got[1:], got[0]))
    small = part // side
    got = [
        lax.ppermute(
            quarter[k * small : (k + 1) * small],
            "row",
            [(2 * side * y + c, 2 * (side * y + k) + c) for y in range(lanes) for c in range(2)],
        )
        for k in range(1, side)
    ]
    return jnp.where(chip % side == 0, quarter[:small], sum(got[1:], got[0]))


def spread_far(piece, cols):
    quarter = cols // 4
    got = [
        lax.ppermute(piece, "col", [(0, quarter * k), (1, quarter * k + 1)]) for k in range(1, 4)
    ]
    return jnp.where(lax.axis_index("col") < 2, piece, got[0] + got[1] + got[2])


def spread_near(held, cols):
    groups = range(0, cols, 4)
    swap = lax.ppermute(held, "col", [p for g in groups for p in ((g, g + 1), (g + 1, g))])
    near = lax.ppermute(held, "col", [p for g in groups for p in ((g, g + 2), (g + 1, g + 3))])
    far = lax.ppermute(held, "col", [p for g in groups for p in ((g, g + 3), (g + 1, g + 2))])
    place = lax.axis_index("col") % 4
    first = jnp.where(place == 0, held, jnp.where(place == 1, swap, jnp.where(place == 2, near, far)))
    second = jnp.where(place == 0, swap, jnp.where(place == 1, held, jnp.where(place == 2, far, near)))
    return jnp.stack([first, second])


def local(matrix, inverses):
    rows, cols = lax.axis_size("row"), lax.axis_size("col")
    size = matrix.shape[0]
    chips = rows // 2
    part = size // chips
    same_core = [[2 * chip + core for chip in range(chips)] for core in range(2)]
    swap_core = [(r, r ^ 1) for r in range(rows)]

    def gather_part(piece):
        copies = jnp.broadcast_to(piece[None], (chips,) + piece.shape)
        return lax.all_to_all(copies, "row", 0, 0, tiled=True, axis_index_groups=same_core)

    with jax.named_scope("panels"):
        held = panel_step(matrix[:, 0, 0, :], 0, cols)
    with jax.named_scope("scatter_rows"):
        dealt = lax.all_to_all(
            matrix, "row", 0, 0, tiled=True, axis_index_groups=same_core
        )[:part, 0]
    first_dealt = dealt
    with jax.named_scope("panels"):
        held = panel_step(held, 1, cols)
    with jax.named_scope("gather_rows"):
        own_rows = gather_part(first_dealt.reshape(part, -1)).reshape(size, -1)
    with jax.named_scope("diagonal"):
        piece = spread_far(dealt[:, 0, :], cols)
    piece, held = lax.optimization_barrier((piece, held))
    with jax.named_scope("panels"):
        held = panel_step(held, 2, cols)
    with jax.named_scope("diagonal"):
        pieces = spread_near(piece, cols)
    pieces, held, own_rows = lax.optimization_barrier((pieces, held, own_rows))
    with jax.named_scope("gather_rows"):
        other_rows = lax.ppermute(own_rows, "row", swap_core)
    with jax.named_scope("diagonal"):
        mine = gather_part(pieces)
    with jax.named_scope("panels"):
        panel = panel_pair(held, cols)
    mine, panel = lax.optimization_barrier((mine, panel))
    late, mine = lax.optimization_barrier((matrix, mine))
    with jax.named_scope("diagonal"):
        other = lax.ppermute(mine, "row", swap_core)
    wide = (size, 2 * size)
    with jax.named_scope("finish"):
        fresh = pl.pallas_call(
            finish_kernel,
            out_shape=jax.ShapeDtypeStruct(wide, jnp.bfloat16),
            in_specs=[whole] * 3 + [pl.BlockSpec(memory_space=pl.ANY)] * 5,
            out_specs=whole,
            scratch_shapes=[pltpu.VMEM(wide, jnp.bfloat16)] * 2
            + [pltpu.VMEM((size, size), jnp.bfloat16)] * 2
            + [pltpu.VMEM(wide, jnp.bfloat16), pltpu.SemaphoreType.DMA((5,))],
            compiler_params=params,
        )(mine, other, inverses, own_rows, other_rows, held, panel, late.reshape(wide))
    return fresh.reshape(matrix.shape)


def solution(mesh):
    return jax.shard_map(
        local,
        mesh=mesh,
        in_specs=(P("row", "col", None, None), P()),
        out_specs=P("row", "col", None, None),
        check_vma=False,
    )
```

```python
import jax
import jax.numpy as jnp
from jax import lax
from jax.experimental import pallas as pl
from jax.experimental.pallas import tpu as pltpu
from jax.sharding import PartitionSpec as P

whole = pl.BlockSpec(memory_space=pltpu.VMEM)
params = pltpu.CompilerParams(vmem_limit_bytes=32 * 1024 * 1024)


def product(left, right):
    return jnp.dot(left, right, preferred_element_type=jnp.float32)


def two_parts(value):
    high = value.astype(jnp.bfloat16)
    return high, (value - high.astype(jnp.float32)).astype(jnp.bfloat16)


def refined_inverse(diagonal, approx):
    size = diagonal.shape[0]
    high, low = two_parts(approx)
    row_ids = lax.broadcasted_iota(jnp.int32, (size, size), 0)
    col_ids = lax.broadcasted_iota(jnp.int32, (size, size), 1)
    twice = jnp.where(row_ids == col_ids, 2.0, 0.0)
    rest_high, rest_low = two_parts(twice - (product(diagonal, high) + product(diagonal, low)))
    small = product(high, rest_low) + product(low, rest_high)
    return (product(high, rest_high) + small).astype(jnp.bfloat16)


def finish_kernel(
    own_diag, other_diag, approx, own_rows, other_rows, held, other, block, out,
    upper0_ref, raw1_ref, panel0_ref, panel1_ref, block_ref, sems,
):
    row, col = lax.axis_index("row"), lax.axis_index("col")
    first, even = row % 2 == 0, col % 2 == 0
    size = out.shape[0]

    def fetch(source, target, index):
        return pltpu.make_async_copy(source, target, sems.at[index])

    @pl.when(first)
    def _():
        fetch(own_rows, upper0_ref, 0).start()
        fetch(other_rows, raw1_ref, 1).start()

    @pl.when(jnp.logical_not(first))
    def _():
        fetch(other_rows, upper0_ref, 0).start()
        fetch(own_rows, raw1_ref, 1).start()

    @pl.when(even)
    def _():
        fetch(held, panel0_ref, 2).start()
        fetch(other, panel1_ref, 3).start()

    @pl.when(jnp.logical_not(even))
    def _():
        fetch(other, panel0_ref, 2).start()
        fetch(held, panel1_ref, 3).start()

    fetch(block, block_ref, 4).start()

    def corner(top, side):
        own, exchanged = own_diag[:, side], other_diag[:, side]
        picked = jnp.where(first, own, exchanged) if top else jnp.where(first, exchanged, own)
        return picked.reshape(size, size)

    inverse0 = refined_inverse(corner(True, 0), approx[0])
    right = corner(True, 1)
    lower10 = product(corner(False, 0), inverse0).astype(jnp.bfloat16)
    upper11 = corner(False, 1).astype(jnp.float32) - product(lower10, right)
    inverse1 = refined_inverse(upper11.astype(jnp.bfloat16), approx[1])
    fetch(own_rows, upper0_ref, 0).wait()
    fetch(own_rows, raw1_ref, 1).wait()
    upper0 = upper0_ref[...]
    upper1 = raw1_ref[...].astype(jnp.float32) - product(lower10, upper0)
    upper1 = upper1.astype(jnp.bfloat16)
    fetch(held, panel0_ref, 2).wait()
    fetch(held, panel1_ref, 3).wait()
    fetch(block, block_ref, 4).wait()
    half = size // 2
    for part in range(2):
        rows = pl.ds(part * half, half)
        lower0 = product(panel0_ref[rows], inverse0).astype(jnp.bfloat16)
        rest = panel1_ref[rows].astype(jnp.float32) - product(lower0, right)
        rest_high, rest_low = two_parts(rest)
        lower1 = product(rest_high, inverse1) + product(rest_low, inverse1)
        lower1 = lower1.astype(jnp.bfloat16)
        used0 = jnp.where(row > 0, lower0, jnp.zeros_like(lower0))
        used1 = jnp.where(row > 1, lower1, jnp.zeros_like(lower1))
        fresh = block_ref[rows].astype(jnp.float32) - product(used0, upper0)
        out[rows] = (fresh - product(used1, upper1)).astype(jnp.bfloat16)

        @pl.when((col == 0) & (row > 0))
        def _():
            out[rows, pl.ds(0, size)] = lower0

        @pl.when((col == 1) & (row > 1))
        def _():
            out[rows, pl.ds(0, size)] = lower1


def panel_step(held, level, cols):
    tree = [[(0, 10)], [(0, 12), (10, 4)], [(0, 2), (4, 6), (10, 8), (12, 14)]][level]
    pairs = tree + [((1 - s) % cols, (1 - t) % cols) for s, t in tree]
    got = lax.ppermute(held, "col", pairs)
    col = lax.axis_index("col")
    arrives = jnp.any(jnp.stack([col == t for _, t in pairs]))
    return jnp.where(arrives, got, held)


def panel_pair(held, cols):
    pairs = [(s, (s - 1) % cols) if s % 2 == 0 else (s, (s + 1) % cols) for s in range(cols)]
    return lax.ppermute(held, "col", pairs)


def deal_rows(block, chips):
    chip, side = lax.axis_index("row") // 2, 4
    lanes = chips // side
    part = block.shape[0] // lanes
    got = [
        lax.ppermute(
            block[k * part : (k + 1) * part], "row", [(c, 2 * side * k + c) for c in range(2)]
        )
        for k in range(1, lanes)
    ]
    quarter = jnp.where(chip // side == 0, block[:part], sum(got[1:], got[0]))
    small = part // side
    got = [
        lax.ppermute(
            quarter[k * small : (k + 1) * small],
            "row",
            [(2 * side * y + c, 2 * (side * y + k) + c) for y in range(lanes) for c in range(2)],
        )
        for k in range(1, side)
    ]
    return jnp.where(chip % side == 0, quarter[:small], sum(got[1:], got[0]))


def spread_far(piece, cols):
    quarter = cols // 4
    got = [
        lax.ppermute(piece, "col", [(0, quarter * k), (1, quarter * k + 1)]) for k in range(1, 4)
    ]
    return jnp.where(lax.axis_index("col") < 2, piece, got[0] + got[1] + got[2])


def spread_near(held, cols):
    groups = range(0, cols, 4)
    swap = lax.ppermute(held, "col", [p for g in groups for p in ((g, g + 1), (g + 1, g))])
    near = lax.ppermute(held, "col", [p for g in groups for p in ((g, g + 2), (g + 1, g + 3))])
    far = lax.ppermute(held, "col", [p for g in groups for p in ((g, g + 3), (g + 1, g + 2))])
    place = lax.axis_index("col") % 4
    first = jnp.where(place == 0, held, jnp.where(place == 1, swap, jnp.where(place == 2, near, far)))
    second = jnp.where(place == 0, swap, jnp.where(place == 1, held, jnp.where(place == 2, far, near)))
    return jnp.stack([first, second])


def local(matrix, inverses):
    rows, cols = lax.axis_size("row"), lax.axis_size("col")
    size = matrix.shape[0]
    chips = rows // 2
    part = size // chips
    same_core = [[2 * chip + core for chip in range(chips)] for core in range(2)]
    swap_core = [(r, r ^ 1) for r in range(rows)]

    def gather_part(piece):
        copies = jnp.broadcast_to(piece[None], (chips,) + piece.shape)
        return lax.all_to_all(copies, "row", 0, 0, tiled=True, axis_index_groups=same_core)

    with jax.named_scope("panels"):
        held = panel_step(matrix[:, 0, 0, :], 0, cols)
    with jax.named_scope("scatter_rows"):
        dealt = lax.all_to_all(
            matrix, "row", 0, 0, tiled=True, axis_index_groups=same_core
        )[:part, 0]
    first_dealt = dealt
    with jax.named_scope("panels"):
        held = panel_step(held, 1, cols)
    with jax.named_scope("gather_rows"):
        own_rows = gather_part(first_dealt.reshape(part, -1)).reshape(size, -1)
    with jax.named_scope("diagonal"):
        piece = spread_far(dealt[:, 0, :], cols)
    piece, held = lax.optimization_barrier((piece, held))
    with jax.named_scope("diagonal"):
        pieces = spread_near(piece, cols)
    pieces, own_rows = lax.optimization_barrier((pieces, own_rows))
    with jax.named_scope("gather_rows"):
        other_rows = lax.ppermute(own_rows, "row", swap_core)
    with jax.named_scope("diagonal"):
        mine = gather_part(pieces)
    with jax.named_scope("panels"):
        held = panel_step(held, 2, cols)
    with jax.named_scope("panels"):
        panel = panel_pair(held, cols)
    mine, panel = lax.optimization_barrier((mine, panel))
    late, mine = lax.optimization_barrier((matrix, mine))
    with jax.named_scope("diagonal"):
        other = lax.ppermute(mine, "row", swap_core)
    wide = (size, 2 * size)
    with jax.named_scope("finish"):
        fresh = pl.pallas_call(
            finish_kernel,
            out_shape=jax.ShapeDtypeStruct(wide, jnp.bfloat16),
            in_specs=[whole] * 3 + [pl.BlockSpec(memory_space=pl.ANY)] * 5,
            out_specs=whole,
            scratch_shapes=[pltpu.VMEM(wide, jnp.bfloat16)] * 2
            + [pltpu.VMEM((size, size), jnp.bfloat16)] * 2
            + [pltpu.VMEM(wide, jnp.bfloat16), pltpu.SemaphoreType.DMA((5,))],
            compiler_params=params,
        )(mine, other, inverses, own_rows, other_rows, held, panel, late.reshape(wide))
    return fresh.reshape(matrix.shape)


def solution(mesh):
    return jax.shard_map(
        local,
        mesh=mesh,
        in_specs=(P("row", "col", None, None), P()),
        out_specs=P("row", "col", None, None),
        check_vma=False,
    )
```

```python
import jax
import jax.numpy as jnp
from jax import lax
from jax.experimental import pallas as pl
from jax.experimental.pallas import tpu as pltpu
from jax.sharding import PartitionSpec as P

whole = pl.BlockSpec(memory_space=pltpu.VMEM)
params = pltpu.CompilerParams(vmem_limit_bytes=32 * 1024 * 1024)


def product(left, right):
    return jnp.dot(left, right, preferred_element_type=jnp.float32)


def two_parts(value):
    high = value.astype(jnp.bfloat16)
    return high, (value - high.astype(jnp.float32)).astype(jnp.bfloat16)


def refined_inverse(diagonal, approx):
    size = diagonal.shape[0]
    high, low = two_parts(approx)
    row_ids = lax.broadcasted_iota(jnp.int32, (size, size), 0)
    col_ids = lax.broadcasted_iota(jnp.int32, (size, size), 1)
    twice = jnp.where(row_ids == col_ids, 2.0, 0.0)
    rest_high, rest_low = two_parts(twice - (product(diagonal, high) + product(diagonal, low)))
    small = product(high, rest_low) + product(low, rest_high)
    return (product(high, rest_high) + small).astype(jnp.bfloat16)


def finish_kernel(
    own_diag, other_diag, approx, own_rows, other_rows, held, other, block, out,
    upper0_ref, raw1_ref, panel0_ref, panel1_ref, block_ref, sems,
):
    row, col = lax.axis_index("row"), lax.axis_index("col")
    first, even = row % 2 == 0, col % 2 == 0
    size = out.shape[0]

    def fetch(source, target, index):
        return pltpu.make_async_copy(source, target, sems.at[index])

    @pl.when(first)
    def _():
        fetch(own_rows, upper0_ref, 0).start()
        fetch(other_rows, raw1_ref, 1).start()

    @pl.when(jnp.logical_not(first))
    def _():
        fetch(other_rows, upper0_ref, 0).start()
        fetch(own_rows, raw1_ref, 1).start()

    @pl.when(even)
    def _():
        fetch(held, panel0_ref, 2).start()
        fetch(other, panel1_ref, 3).start()

    @pl.when(jnp.logical_not(even))
    def _():
        fetch(other, panel0_ref, 2).start()
        fetch(held, panel1_ref, 3).start()

    fetch(block, block_ref, 4).start()

    def corner(top, side):
        own, exchanged = own_diag[:, side], other_diag[:, side]
        picked = jnp.where(first, own, exchanged) if top else jnp.where(first, exchanged, own)
        return picked.reshape(size, size)

    inverse0 = refined_inverse(corner(True, 0), approx[0])
    right = corner(True, 1)
    lower10 = product(corner(False, 0), inverse0).astype(jnp.bfloat16)
    upper11 = corner(False, 1).astype(jnp.float32) - product(lower10, right)
    inverse1 = refined_inverse(upper11.astype(jnp.bfloat16), approx[1])
    fetch(own_rows, upper0_ref, 0).wait()
    fetch(own_rows, raw1_ref, 1).wait()
    upper0 = upper0_ref[...]
    upper1 = raw1_ref[...].astype(jnp.float32) - product(lower10, upper0)
    upper1 = upper1.astype(jnp.bfloat16)
    fetch(held, panel0_ref, 2).wait()
    fetch(held, panel1_ref, 3).wait()
    fetch(block, block_ref, 4).wait()
    half = size // 2
    for part in range(2):
        rows = pl.ds(part * half, half)
        lower0 = product(panel0_ref[rows], inverse0).astype(jnp.bfloat16)
        rest = panel1_ref[rows].astype(jnp.float32) - product(lower0, right)
        rest_high, rest_low = two_parts(rest)
        lower1 = product(rest_high, inverse1) + product(rest_low, inverse1)
        lower1 = lower1.astype(jnp.bfloat16)
        used0 = jnp.where(row > 0, lower0, jnp.zeros_like(lower0))
        used1 = jnp.where(row > 1, lower1, jnp.zeros_like(lower1))
        fresh = block_ref[rows].astype(jnp.float32) - product(used0, upper0)
        out[rows] = (fresh - product(used1, upper1)).astype(jnp.bfloat16)

        @pl.when((col == 0) & (row > 0))
        def _():
            out[rows, pl.ds(0, size)] = lower0

        @pl.when((col == 1) & (row > 1))
        def _():
            out[rows, pl.ds(0, size)] = lower1


def panel_step(held, level, cols):
    tree = [[(0, 10)], [(0, 12), (10, 4)], [(0, 2), (4, 6), (10, 8), (12, 14)]][level]
    pairs = tree + [((1 - s) % cols, (1 - t) % cols) for s, t in tree]
    got = lax.ppermute(held, "col", pairs)
    col = lax.axis_index("col")
    arrives = jnp.any(jnp.stack([col == t for _, t in pairs]))
    return jnp.where(arrives, got, held)


def panel_pair(held, cols):
    pairs = [(s, (s - 1) % cols) if s % 2 == 0 else (s, (s + 1) % cols) for s in range(cols)]
    return lax.ppermute(held, "col", pairs)


def deal_rows(block, chips):
    chip, side = lax.axis_index("row") // 2, 4
    lanes = chips // side
    part = block.shape[0] // lanes
    got = [
        lax.ppermute(
            block[k * part : (k + 1) * part], "row", [(c, 2 * side * k + c) for c in range(2)]
        )
        for k in range(1, lanes)
    ]
    quarter = jnp.where(chip // side == 0, block[:part], sum(got[1:], got[0]))
    small = part // side
    got = [
        lax.ppermute(
            quarter[k * small : (k + 1) * small],
            "row",
            [(2 * side * y + c, 2 * (side * y + k) + c) for y in range(lanes) for c in range(2)],
        )
        for k in range(1, side)
    ]
    return jnp.where(chip % side == 0, quarter[:small], sum(got[1:], got[0]))


def spread_far(piece, cols):
    quarter = cols // 4
    got = [
        lax.ppermute(piece, "col", [(0, quarter * k), (1, quarter * k + 1)]) for k in range(1, 4)
    ]
    return jnp.where(lax.axis_index("col") < 2, piece, got[0] + got[1] + got[2])


def spread_near(held, cols):
    groups = range(0, cols, 4)
    swap = lax.ppermute(held, "col", [p for g in groups for p in ((g, g + 1), (g + 1, g))])
    near = lax.ppermute(held, "col", [p for g in groups for p in ((g, g + 2), (g + 1, g + 3))])
    far = lax.ppermute(held, "col", [p for g in groups for p in ((g, g + 3), (g + 1, g + 2))])
    place = lax.axis_index("col") % 4
    first = jnp.where(place == 0, held, jnp.where(place == 1, swap, jnp.where(place == 2, near, far)))
    second = jnp.where(place == 0, swap, jnp.where(place == 1, held, jnp.where(place == 2, far, near)))
    return jnp.stack([first, second])


def local(matrix, inverses):
    rows, cols = lax.axis_size("row"), lax.axis_size("col")
    size = matrix.shape[0]
    chips = rows // 2
    part = size // chips
    same_core = [[2 * chip + core for chip in range(chips)] for core in range(2)]
    swap_core = [(r, r ^ 1) for r in range(rows)]

    def gather_part(piece):
        copies = jnp.broadcast_to(piece[None], (chips,) + piece.shape)
        return lax.all_to_all(copies, "row", 0, 0, tiled=True, axis_index_groups=same_core)

    with jax.named_scope("panels"):
        held = panel_step(matrix[:, 0, 0, :], 0, cols)
    with jax.named_scope("scatter_rows"):
        dealt = lax.all_to_all(
            matrix, "row", 0, 0, tiled=True, axis_index_groups=same_core
        )[:part, 0]
    first_dealt = dealt
    with jax.named_scope("panels"):
        held = panel_step(held, 1, cols)
    with jax.named_scope("gather_rows"):
        own_rows = gather_part(first_dealt.reshape(part, -1)).reshape(size, -1)
    with jax.named_scope("diagonal"):
        piece = spread_far(dealt[:, 0, :], cols)
    with jax.named_scope("diagonal"):
        pieces = spread_near(piece, cols)
    pieces, own_rows, held = lax.optimization_barrier((pieces, own_rows, held))
    with jax.named_scope("gather_rows"):
        other_rows = lax.ppermute(own_rows, "row", swap_core)
    with jax.named_scope("diagonal"):
        mine = gather_part(pieces)
    with jax.named_scope("panels"):
        held = panel_step(held, 2, cols)
    with jax.named_scope("panels"):
        panel = panel_pair(held, cols)
    mine, panel = lax.optimization_barrier((mine, panel))
    late, mine = lax.optimization_barrier((matrix, mine))
    with jax.named_scope("diagonal"):
        other = lax.ppermute(mine, "row", swap_core)
    wide = (size, 2 * size)
    with jax.named_scope("finish"):
        fresh = pl.pallas_call(
            finish_kernel,
            out_shape=jax.ShapeDtypeStruct(wide, jnp.bfloat16),
            in_specs=[whole] * 3 + [pl.BlockSpec(memory_space=pl.ANY)] * 5,
            out_specs=whole,
            scratch_shapes=[pltpu.VMEM(wide, jnp.bfloat16)] * 2
            + [pltpu.VMEM((size, size), jnp.bfloat16)] * 2
            + [pltpu.VMEM(wide, jnp.bfloat16), pltpu.SemaphoreType.DMA((5,))],
            compiler_params=params,
        )(mine, other, inverses, own_rows, other_rows, held, panel, late.reshape(wide))
    return fresh.reshape(matrix.shape)


def solution(mesh):
    return jax.shard_map(
        local,
        mesh=mesh,
        in_specs=(P("row", "col", None, None), P()),
        out_specs=P("row", "col", None, None),
        check_vma=False,
    )
```

```python
import jax
import jax.numpy as jnp
from jax import lax
from jax.experimental import pallas as pl
from jax.experimental.pallas import tpu as pltpu
from jax.sharding import PartitionSpec as P

whole = pl.BlockSpec(memory_space=pltpu.VMEM)
params = pltpu.CompilerParams(vmem_limit_bytes=32 * 1024 * 1024)


def product(left, right):
    return jnp.dot(left, right, preferred_element_type=jnp.float32)


def two_parts(value):
    high = value.astype(jnp.bfloat16)
    return high, (value - high.astype(jnp.float32)).astype(jnp.bfloat16)


def refined_inverse(diagonal, approx):
    size = diagonal.shape[0]
    high, low = two_parts(approx)
    row_ids = lax.broadcasted_iota(jnp.int32, (size, size), 0)
    col_ids = lax.broadcasted_iota(jnp.int32, (size, size), 1)
    twice = jnp.where(row_ids == col_ids, 2.0, 0.0)
    rest_high, rest_low = two_parts(twice - (product(diagonal, high) + product(diagonal, low)))
    small = product(high, rest_low) + product(low, rest_high)
    return (product(high, rest_high) + small).astype(jnp.bfloat16)


def finish_kernel(
    own_diag, other_diag, approx, own_rows, other_rows, held, other, block, out,
    upper0_ref, raw1_ref, panel0_ref, panel1_ref, block_ref, sems,
):
    row, col = lax.axis_index("row"), lax.axis_index("col")
    first, even = row % 2 == 0, col % 2 == 0
    size = out.shape[0]

    def fetch(source, target, index):
        return pltpu.make_async_copy(source, target, sems.at[index])

    @pl.when(first)
    def _():
        fetch(own_rows, upper0_ref, 0).start()
        fetch(other_rows, raw1_ref, 1).start()

    @pl.when(jnp.logical_not(first))
    def _():
        fetch(other_rows, upper0_ref, 0).start()
        fetch(own_rows, raw1_ref, 1).start()

    @pl.when(even)
    def _():
        fetch(held, panel0_ref, 2).start()
        fetch(other, panel1_ref, 3).start()

    @pl.when(jnp.logical_not(even))
    def _():
        fetch(other, panel0_ref, 2).start()
        fetch(held, panel1_ref, 3).start()

    fetch(block, block_ref, 4).start()

    def corner(top, side):
        own, exchanged = own_diag[:, side], other_diag[:, side]
        picked = jnp.where(first, own, exchanged) if top else jnp.where(first, exchanged, own)
        return picked.reshape(size, size)

    inverse0 = refined_inverse(corner(True, 0), approx[0])
    right = corner(True, 1)
    lower10 = product(corner(False, 0), inverse0).astype(jnp.bfloat16)
    upper11 = corner(False, 1).astype(jnp.float32) - product(lower10, right)
    inverse1 = refined_inverse(upper11.astype(jnp.bfloat16), approx[1])
    fetch(own_rows, upper0_ref, 0).wait()
    fetch(own_rows, raw1_ref, 1).wait()
    upper0 = upper0_ref[...]
    upper1 = raw1_ref[...].astype(jnp.float32) - product(lower10, upper0)
    upper1 = upper1.astype(jnp.bfloat16)
    fetch(held, panel0_ref, 2).wait()
    fetch(held, panel1_ref, 3).wait()
    fetch(block, block_ref, 4).wait()
    half = size
    for part in range(1):
        rows = pl.ds(part * half, half)
        lower0 = product(panel0_ref[rows], inverse0).astype(jnp.bfloat16)
        rest = panel1_ref[rows].astype(jnp.float32) - product(lower0, right)
        rest_high, rest_low = two_parts(rest)
        lower1 = product(rest_high, inverse1) + product(rest_low, inverse1)
        lower1 = lower1.astype(jnp.bfloat16)
        used0 = jnp.where(row > 0, lower0, jnp.zeros_like(lower0))
        used1 = jnp.where(row > 1, lower1, jnp.zeros_like(lower1))
        fresh = block_ref[rows].astype(jnp.float32) - product(used0, upper0)
        out[rows] = (fresh - product(used1, upper1)).astype(jnp.bfloat16)

        @pl.when((col == 0) & (row > 0))
        def _():
            out[rows, pl.ds(0, size)] = lower0

        @pl.when((col == 1) & (row > 1))
        def _():
            out[rows, pl.ds(0, size)] = lower1


def panel_step(held, level, cols):
    tree = [[(0, 10)], [(0, 12), (10, 4)], [(0, 2), (4, 6), (10, 8), (12, 14)]][level]
    pairs = tree + [((1 - s) % cols, (1 - t) % cols) for s, t in tree]
    got = lax.ppermute(held, "col", pairs)
    col = lax.axis_index("col")
    arrives = jnp.any(jnp.stack([col == t for _, t in pairs]))
    return jnp.where(arrives, got, held)


def panel_pair(held, cols):
    pairs = [(s, (s - 1) % cols) if s % 2 == 0 else (s, (s + 1) % cols) for s in range(cols)]
    return lax.ppermute(held, "col", pairs)


def deal_rows(block, chips):
    chip, side = lax.axis_index("row") // 2, 4
    lanes = chips // side
    part = block.shape[0] // lanes
    got = [
        lax.ppermute(
            block[k * part : (k + 1) * part], "row", [(c, 2 * side * k + c) for c in range(2)]
        )
        for k in range(1, lanes)
    ]
    quarter = jnp.where(chip // side == 0, block[:part], sum(got[1:], got[0]))
    small = part // side
    got = [
        lax.ppermute(
            quarter[k * small : (k + 1) * small],
            "row",
            [(2 * side * y + c, 2 * (side * y + k) + c) for y in range(lanes) for c in range(2)],
        )
        for k in range(1, side)
    ]
    return jnp.where(chip % side == 0, quarter[:small], sum(got[1:], got[0]))


def spread_far(piece, cols):
    quarter = cols // 4
    got = [
        lax.ppermute(piece, "col", [(0, quarter * k), (1, quarter * k + 1)]) for k in range(1, 4)
    ]
    return jnp.where(lax.axis_index("col") < 2, piece, got[0] + got[1] + got[2])


def spread_near(held, cols):
    groups = range(0, cols, 4)
    swap = lax.ppermute(held, "col", [p for g in groups for p in ((g, g + 1), (g + 1, g))])
    near = lax.ppermute(held, "col", [p for g in groups for p in ((g, g + 2), (g + 1, g + 3))])
    far = lax.ppermute(held, "col", [p for g in groups for p in ((g, g + 3), (g + 1, g + 2))])
    place = lax.axis_index("col") % 4
    first = jnp.where(place == 0, held, jnp.where(place == 1, swap, jnp.where(place == 2, near, far)))
    second = jnp.where(place == 0, swap, jnp.where(place == 1, held, jnp.where(place == 2, far, near)))
    return jnp.stack([first, second])


def local(matrix, inverses):
    rows, cols = lax.axis_size("row"), lax.axis_size("col")
    size = matrix.shape[0]
    chips = rows // 2
    part = size // chips
    same_core = [[2 * chip + core for chip in range(chips)] for core in range(2)]
    swap_core = [(r, r ^ 1) for r in range(rows)]

    def gather_part(piece):
        copies = jnp.broadcast_to(piece[None], (chips,) + piece.shape)
        return lax.all_to_all(copies, "row", 0, 0, tiled=True, axis_index_groups=same_core)

    with jax.named_scope("panels"):
        held = panel_step(matrix[:, 0, 0, :], 0, cols)
    with jax.named_scope("scatter_rows"):
        dealt = lax.all_to_all(
            matrix, "row", 0, 0, tiled=True, axis_index_groups=same_core
        )[:part, 0]
    first_dealt = dealt
    with jax.named_scope("panels"):
        held = panel_step(held, 1, cols)
    with jax.named_scope("gather_rows"):
        own_rows = gather_part(first_dealt.reshape(part, -1)).reshape(size, -1)
    with jax.named_scope("diagonal"):
        piece = spread_far(dealt[:, 0, :], cols)
    with jax.named_scope("diagonal"):
        pieces = spread_near(piece, cols)
    pieces, own_rows, held = lax.optimization_barrier((pieces, own_rows, held))
    with jax.named_scope("gather_rows"):
        other_rows = lax.ppermute(own_rows, "row", swap_core)
    with jax.named_scope("diagonal"):
        mine = gather_part(pieces)
    with jax.named_scope("panels"):
        held = panel_step(held, 2, cols)
    with jax.named_scope("panels"):
        panel = panel_pair(held, cols)
    mine, panel = lax.optimization_barrier((mine, panel))
    late, mine = lax.optimization_barrier((matrix, mine))
    with jax.named_scope("diagonal"):
        other = lax.ppermute(mine, "row", swap_core)
    wide = (size, 2 * size)
    with jax.named_scope("finish"):
        fresh = pl.pallas_call(
            finish_kernel,
            out_shape=jax.ShapeDtypeStruct(wide, jnp.bfloat16),
            in_specs=[whole] * 3 + [pl.BlockSpec(memory_space=pl.ANY)] * 5,
            out_specs=whole,
            scratch_shapes=[pltpu.VMEM(wide, jnp.bfloat16)] * 2
            + [pltpu.VMEM((size, size), jnp.bfloat16)] * 2
            + [pltpu.VMEM(wide, jnp.bfloat16), pltpu.SemaphoreType.DMA((5,))],
            compiler_params=params,
        )(mine, other, inverses, own_rows, other_rows, held, panel, late.reshape(wide))
    return fresh.reshape(matrix.shape)


def solution(mesh):
    return jax.shard_map(
        local,
        mesh=mesh,
        in_specs=(P("row", "col", None, None), P()),
        out_specs=P("row", "col", None, None),
        check_vma=False,
    )
```
